32 devices in a mesh: row: 8 (over y, x, core), col: 4 (over z).
Axes of the slice: x: 2, y: 2, z: 4, core: 2. Of those that a mesh axis runs over, the one named last changes fastest.
Arguments:
- vectors_in: float32 [4096, 1024], P('row', 'col'), may hold values from -6 to 6
- poles_one: float32 [2, 2048], replicated, may hold values from 0 to 2048, as said below
- roots_one: float32 [2, 2048], replicated, may hold values from 0 to 2048, as said below
- order_one: int32 [2, 2048], replicated, may hold values from 0 to 2047, each once within a row
- deflate_one: int32 [2, 2048], replicated, may hold values 0 or 1
- poles_two: float32 [4096], replicated, may hold values from 0 to 4096, as said below
- roots_two: float32 [4096], replicated, may hold values from 0 to 4096, as said below
- order_two: int32 [4096], replicated, may hold values from 0 to 4095, each once
- deflate_two: int32 [4096], replicated, may hold values 0 or 1
Outputs:
- merged: float32 [4096, 4096], P('row', 'col')
The draws below stay inside these ranges and needn't reach their ends.
Inputs may be any that keep to these rules, and one draw needn't show every extreme that they name: `poles_one`: along the last dimension, the entry at position k lies between k and k + 0.3. `roots_one`: along the last dimension, the entry at position k lies between k + 0.45 and k + 0.75. `poles_two`: the entry at position k lies between k and k + 0.3. `roots_two`: the entry at position k lies between k + 0.45 and k + 0.75.
All inputs are finite; a program needn't handle non-finite values.
Results may differ from the reference program's by a relative error of at most 0.0003.
Values sent between devices are 32-bit elements; how exact they have to be, the bound alone decides.
No kernel may reach another device: no remote copies, remote signals or barrier semaphores. Data moves between devices by JAX's collectives and lax.ppermute only.
A program may use at most 64 MiB of HBM per device.

```python
import jax
import jax.numpy as jnp
from jax import lax

LEAF_COLS = 1024
ROWS = 4096


def draw_poles_one(key, part):
    key = jax.random.fold_in(key, 11)
    unit = jax.random.uniform(key, (2, 2 * LEAF_COLS), jnp.float32)
    return jnp.arange(2 * LEAF_COLS, dtype=jnp.float32)[None, :] + 0.3 * unit


def draw_roots_one(key, part):
    key = jax.random.fold_in(key, 23)
    unit = jax.random.uniform(key, (2, 2 * LEAF_COLS), jnp.float32)
    return jnp.arange(2 * LEAF_COLS, dtype=jnp.float32)[None, :] + 0.45 + 0.3 * unit


def draw_poles_two(key, part):
    key = jax.random.fold_in(key, 37)
    unit = jax.random.uniform(key, (4 * LEAF_COLS,), jnp.float32)
    return jnp.arange(4 * LEAF_COLS, dtype=jnp.float32) + 0.3 * unit


def draw_roots_two(key, part):
    key = jax.random.fold_in(key, 41)
    unit = jax.random.uniform(key, (4 * LEAF_COLS,), jnp.float32)
    return jnp.arange(4 * LEAF_COLS, dtype=jnp.float32) + 0.45 + 0.3 * unit


def plant(values, own_key, least, high):
    place = [jax.random.randint(jax.random.fold_in(own_key, axis), (), 0, length) for axis, length in enumerate(values.shape)]
    main_axis = values.shape.index(max(values.shape))
    beside = place[:main_axis] + [(place[main_axis] + 1) % values.shape[main_axis]] + place[main_axis + 1:]
    return values.at[tuple(place)].set(least).at[tuple(beside)].set(high)


def block_levels(key, shape, cuts, least, largest):
    def one(dim, blocks):
        draws = jax.random.uniform(jax.random.fold_in(jax.random.fold_in(key, 6), dim), (blocks,), jnp.float32, least / len(cuts), largest / len(cuts))
        return jnp.repeat(jnp.exp(draws), shape[dim] // blocks).reshape((-1,) + (1,) * (len(shape) - dim - 1))

    factor_of = one(*cuts[0])
    for cut in cuts[1:]:
        factor_of = factor_of * one(*cut)
    return factor_of


def gaussian(own_key, shape, spread, reach, split=(), kind=jnp.bfloat16):
    loudness = block_levels(own_key, shape, split, -0.22, 0.18) if split else 1.0
    values = jax.random.normal(own_key, shape, jnp.float32) * spread * loudness
    return jnp.minimum(jnp.maximum(values, -reach), reach).astype(kind)


def setup_inputs(seed: int = 0) -> dict:
    seeds = jax.random.split(jax.random.key(seed), 10)
    return {
        "vectors_in": gaussian(seeds[0], (ROWS, LEAF_COLS), 1.0, 6.0, ((0, 8), (1, 4)), jnp.float32),
        "poles_one": draw_poles_one(jax.random.fold_in(seeds[9], 71), 0),
        "roots_one": draw_roots_one(jax.random.fold_in(seeds[9], 71), 0),
        "order_one": jax.vmap(lambda own: jax.random.permutation(own, 2 * LEAF_COLS))(jax.random.split(seeds[3], 2)).reshape((2, 2 * LEAF_COLS)).astype(jnp.int32),
        "deflate_one": plant((jax.random.randint(seeds[4], (2, 2 * LEAF_COLS), 0, 4) < 1).astype(jnp.int32), jax.random.fold_in(seeds[4], 1), 0, 1),
        "poles_two": draw_poles_two(jax.random.fold_in(seeds[9], 71), 0),
        "roots_two": draw_roots_two(jax.random.fold_in(seeds[9], 71), 0),
        "order_two": jax.random.permutation(seeds[7], 4 * LEAF_COLS).astype(jnp.int32),
        "deflate_two": plant((jax.random.randint(seeds[8], (4 * LEAF_COLS,), 0, 4) < 1).astype(jnp.int32), jax.random.fold_in(seeds[8], 1), 0, 1),
    }


def merge_level(upper, lower, z_full, pole_vals, root_vals, order_vals, deflate):
    level_size = pole_vals.shape[0]
    half_size = level_size // 2
    inverse = jnp.argsort(order_vals).astype(jnp.int32)
    kept_mask = (1 - deflate).astype(jnp.float32)
    dropped = deflate.astype(jnp.float32)
    kept_rows = kept_mask[inverse]
    cauchy = z_full[:, None] / (pole_vals[inverse][:, None] - root_vals[None, :])
    scales = lax.rsqrt(lax.optimization_barrier(jnp.sum(kept_rows[:, None] * cauchy * cauchy, axis=0)) + 1e-06)
    matches = (inverse[:, None] == jnp.arange(level_size, dtype=jnp.int32)[None, :]).astype(jnp.float32)
    factors = kept_rows[:, None] * (1.0 - dropped)[None, :] * cauchy * scales[None, :] + dropped[None, :] * matches
    top_part = jnp.dot(upper, factors[:half_size], precision=lax.Precision.HIGHEST, preferred_element_type=jnp.float32)
    low_part = jnp.dot(lower, factors[half_size:], precision=lax.Precision.HIGHEST, preferred_element_type=jnp.float32)
    return jnp.concatenate([top_part, low_part], axis=0)

def reference(vectors_in, poles_one, roots_one, order_one, deflate_one, poles_two, roots_two, order_two, deflate_two):
    quarters = vectors_in.reshape(4, ROWS // 4, LEAF_COLS)
    pair_blocks = []
    for which in range(2):
        upper = quarters[2 * which]
        lower = quarters[2 * which + 1]
        z_one = jnp.concatenate([upper[-1], lower[0]])
        pair_blocks.append(merge_level(upper, lower, z_one, poles_one[which], roots_one[which], order_one[which], deflate_one[which]))
    z_two = jnp.concatenate([pair_blocks[0][-1], pair_blocks[1][0]])
    return merge_level(pair_blocks[0], pair_blocks[1], z_two, poles_two, roots_two, order_two, deflate_two)
```

```python
import functools
import math

import jax
import jax.numpy as jnp
from jax import lax
from jax.experimental import pallas as pl
from jax.experimental.pallas import tpu as pltpu
from jax.sharding import PartitionSpec as P

F32 = jnp.float32
BF16 = jnp.bfloat16
LANES = 128
SOME_VMEM = 14 * 1024 * 1024
ROWS, WIDTH = 32, 512


def split(x):
    high = x.astype(BF16)
    return high, (x - high.astype(F32)).astype(BF16)


def dot3(a_high, a_low, b_high, b_low):
    dot = functools.partial(jnp.dot, preferred_element_type=F32)
    return dot(a_high, b_high) + dot(a_low, b_high) + dot(a_high, b_low)


def as_columns(row):
    count = row.shape[1] // LANES
    stacked = jnp.concatenate([row[:, LANES * b : LANES * (b + 1)] for b in range(count)], axis=0)
    return stacked.T


def permuted(order, low_bits, wanted, values):
    at_high = order >> 7 == wanted
    at_low = ((order & 127) == low_bits).astype(BF16)
    rows = jnp.concatenate([jnp.where(at_high, v, 0.0).astype(BF16) for v in values], axis=0)
    out = lax.dot_general(rows, at_low, (((1,), (1,)), ((), ())), preferred_element_type=F32)
    count = wanted.shape[0]
    return [out[count * i : count * (i + 1)] for i in range(len(values))]


def place_tables(order, poles, flags, wanted):
    span = order.shape[1]
    low_bits = lax.broadcasted_iota(jnp.int32, (LANES, span), 0)
    index = lax.broadcasted_iota(jnp.int32, (1, span), 1)
    first = poles.astype(BF16).astype(F32)
    second = (poles - first).astype(BF16).astype(F32)
    third = poles - first - second
    values = [first, second, third, (index >> 6).astype(F32), (index & 63).astype(F32), flags.astype(F32)]
    one, two, three, upper, lower, flag = permuted(order, low_bits, wanted, values)
    gone = flag > 0.5
    pole = jnp.where(gone, jnp.inf, one + two + three)
    target = jnp.where(gone, upper * 64.0 + lower, -1.0)
    return pole, target


def perm_kernel(place, order_one, poles_one, flags_one, order_two, poles_two, flags_two, one_out, two_out):
    pair, side, piece = place[0], place[1], place[2]
    blocks = 2 * place_blocks(order_one)
    spot = lax.broadcasted_iota(jnp.int32, (blocks, 1), 0)
    half = blocks // 2
    per = half // 4
    wanted_one = jnp.where(spot >= half, 1 - side, side) * half + (((spot % half) // per) ^ piece) * per + spot % per
    at = pl.ds(pair, 1)
    pole, target = place_tables(order_one[at, :], poles_one[at, :], flags_one[at, :], wanted_one)
    one_out[...] = jnp.concatenate([pole, target], axis=0).T
    pole, target = place_tables(order_two[...], poles_two[...], flags_two[...], spot + pair * blocks)
    two_out[...] = jnp.concatenate([pole, target], axis=0).T


def place_blocks(order_one):
    return order_one.shape[1] // (2 * LANES)


def kept_roots(roots, flags):
    return jnp.where(flags > 0, -jnp.inf, roots)


def inverse_gap(pole, target, roots, index):
    gap = pltpu.reciprocal(pole - roots, approx=True)
    return jnp.where(target == index, 1.0, gap)


def over_tiles(height, width, tile):
    for first in range(0, width, WIDTH):
        lanes = slice(first, first + WIDTH)
        for b in range(height // LANES):

            def step(i, _, b=b, lanes=lanes):
                near = pl.multiple_of(i * ROWS, ROWS)
                tile(b, pl.ds(near, ROWS), pl.ds(pl.multiple_of(b * LANES + near, ROWS), ROWS), lanes)
                return 0

            lax.fori_loop(0, LANES // ROWS, step, 0, unroll=LANES // ROWS)


def table_one_kernel(place, cols_ref, roots_ref, flags_ref, high_ref, low_ref):
    at = pl.ds(place[0], 1)
    roots = kept_roots(roots_ref[at, :], flags_ref[at, :])
    index = lax.broadcasted_iota(jnp.int32, roots.shape, 1).astype(F32)
    blocks = cols_ref.shape[1] // 2

    def tile(b, near, rows, lanes):
        pole, target = cols_ref[near, b : b + 1], cols_ref[near, blocks + b : blocks + b + 1]
        high_ref[rows, lanes], low_ref[rows, lanes] = split(inverse_gap(pole, target, roots[:, lanes], index[:, lanes]))

    over_tiles(*high_ref.shape, tile)


def table_two_kernel(place, cols_ref, roots_ref, flags_ref, out_ref):
    columns = out_ref.shape[1]
    first = pl.multiple_of(place[2] * columns, LANES)
    roots = kept_roots(roots_ref[:, pl.ds(first, columns)], flags_ref[:, pl.ds(first, columns)])
    index = (lax.broadcasted_iota(jnp.int32, roots.shape, 1) + first).astype(F32)
    blocks = cols_ref.shape[1] // 2

    def tile(b, near, rows, lanes):
        pole, target = cols_ref[near, b : b + 1], cols_ref[near, blocks + b : blocks + b + 1]
        out_ref[rows, lanes] = inverse_gap(pole, target, roots[:, lanes], index[:, lanes])

    over_tiles(*out_ref.shape, tile)


def add_rows(total, x):
    for i in range(0, x.shape[0], 8):
        total = total + x[i : i + 8]
    return total


def norm_one_kernel(place, edge_ref, cols_ref, roots_ref, flags_ref, out_ref, edge_cols):
    pair, side = place[0], place[1]
    at = pl.ds(pair, 1)
    roots = kept_roots(roots_ref[at, :], flags_ref[at, :])
    width = roots.shape[1]
    index = lax.broadcasted_iota(jnp.int32, roots.shape, 1).astype(F32)
    blocks = cols_ref.shape[1] // 2
    edges = edge_ref[...]
    share = edges.shape[1]
    own = jnp.where(side == 0, edges[0:1], edges[1:2])
    other = jnp.where(side == 0, edges[1:2], edges[0:1])
    own_edge = jnp.where(side == 1 - pair, edges[2:3], 0.0)
    other_edge = jnp.where(side == 1 - pair, 0.0, edges[2:3])
    pad = jnp.zeros((4, share), F32)
    rows_all = jnp.concatenate([own, other, own_edge, other_edge, pad], axis=0)
    for b in range(share // LANES):
        edge_cols[b] = rows_all[:, LANES * b : LANES * (b + 1)].T
    for first in range(0, width, WIDTH):
        lanes = slice(first, first + WIDTH)
        carry = (jnp.zeros((8, WIDTH), F32), jnp.zeros((8, WIDTH), F32))
        for part in range(2):
            for b in range(share // LANES):
                block = part * (blocks // 2) + b

                def step(i, carry, part=part, b=b, block=block, lanes=lanes):
                    rows = pl.ds(pl.multiple_of(i * ROWS, ROWS), ROWS)
                    target = cols_ref[rows, blocks + block : blocks + block + 1]
                    gap = pltpu.reciprocal(cols_ref[rows, block : block + 1] - roots[:, lanes], approx=True)
                    z = edge_cols[b, rows, part : part + 1]
                    edge = edge_cols[b, rows, 2 + part : 3 + part]
                    scaled = z * gap
                    weighed = edge * jnp.where(target == index[:, lanes], 1.0, scaled)
                    return add_rows(carry[0], scaled * scaled), add_rows(carry[1], weighed)

                carry = lax.fori_loop(0, LANES // ROWS, step, carry, unroll=LANES // ROWS)
        out_ref[0:1, lanes] = jnp.sum(carry[0], axis=0, keepdims=True)
        out_ref[1:2, lanes] = jnp.sum(carry[1], axis=0, keepdims=True)
    out_ref[2:3, :] = jnp.concatenate([own, jnp.zeros((1, width - share), F32)], axis=1)
    out_ref[3:4, :] = jnp.zeros((1, width), F32)


def weight_kernel(place, here, near, far, last, flags_ref, one_cols, two_cols, out_ref):
    pieces = [here, near, far, last]
    share = here.shape[1] // 8
    squares = sum(p[0:1, :] for p in pieces)
    edge = sum(p[1:2, :] for p in pieces)
    gone = flags_ref[pl.ds(place[0], 1), :] > 0
    scale = jnp.where(gone, 1.0, lax.rsqrt(squares + 1e-06))
    blocks = two_cols.shape[1] // 2
    scale = as_columns(scale)
    z_two = as_columns(edge) * scale
    row_gone = two_cols[:, blocks:] >= 0.0
    out_ref[:, 0:blocks] = scale * jnp.where(row_gone, 1.0, z_two)
    out_ref[:, blocks : 2 * blocks] = jnp.where(row_gone, 0.0, z_two)
    z_one = as_columns(jnp.concatenate([p[2:3, 0:share] for p in pieces], axis=1))
    row_gone = one_cols[:, blocks : blocks + blocks // 2] >= 0.0
    out_ref[:, 2 * blocks : 2 * blocks + blocks // 2] = jnp.where(row_gone, 1.0, z_one)


def mid_kernel(part, weights, high_ref, low_ref, two_ref, mid_high, mid_low, squares_ref, b_high, b_low):
    depth, columns = b_high.shape
    blocks = depth // LANES
    for first in range(0, columns, WIDTH):
        lanes = slice(first, first + WIDTH)
        from_lanes = slice(part * columns + first, part * columns + first + WIDTH)
        squares = jnp.zeros((8, WIDTH), F32)
        for b in range(blocks):

            def step(i, squares, b=b, lanes=lanes, from_lanes=from_lanes):
                rows = pl.ds(pl.multiple_of(i * ROWS, ROWS), ROWS)
                to = pl.ds(pl.multiple_of(b * LANES + i * ROWS, ROWS), ROWS)
                table = two_ref[to, from_lanes]
                b_high[to, lanes], b_low[to, lanes] = split(table * weights[rows, b : b + 1])
                scaled = table * weights[rows, blocks + b : blocks + b + 1]
                return add_rows(squares, scaled * scaled)

            squares = lax.fori_loop(0, LANES // ROWS, step, squares, unroll=LANES // ROWS)
        squares_ref[:, lanes] = jnp.sum(squares, axis=0, keepdims=True)
    for b in range(mid_high.shape[0] // 256):
        rows = slice(256 * b, 256 * (b + 1))
        mid = dot3(high_ref[rows, :], low_ref[rows, :], b_high[...], b_low[...])
        for part in range(2):
            at = 2 * blocks + 2 * b + part
            to = slice(256 * b + LANES * part, 256 * b + LANES * (part + 1))
            mid_high[to, :], mid_low[to, :] = split(mid[LANES * part : LANES * (part + 1)] * weights[:, at : at + 1])


def apply_kernel(count, *refs):
    pieces, (left_high, left_low, right_high, right_low, out_ref) = refs[:count], refs[count:]
    share = pieces[0].shape[1]
    for i, (mid_high, mid_low) in enumerate(((left_high, left_low), (right_high, right_low))):
        width = mid_high.shape[1]
        total = None
        for k, piece in enumerate(pieces):
            rows = slice(share * k, share * (k + 1))
            term = dot3(*split(piece[...]), mid_high[rows, :], mid_low[rows, :])
            total = term if total is None else total + term
        out_ref[:, width * i : width * (i + 1)] = total


def finish_kernel(place, total_ref, mine, other, squares_left, squares_right, squares_far, flags_ref,
                  left_high, left_low, right_high, right_low, out_ref):
    columns = out_ref.shape[1]
    share = mine.shape[1]
    flags = flags_ref[:, pl.ds(pl.multiple_of(place[2] * columns, LANES), columns)]
    squares = jnp.concatenate([squares_left[...], squares_right[...]], axis=1) + squares_far[...]
    scale = jnp.where(flags > 0, 1.0, lax.rsqrt(squares + 1e-06))
    high, low = split(mine[...] + other[...])
    for i, (mid_high, mid_low) in enumerate(((left_high, left_low), (right_high, right_low))):
        width = mid_high.shape[1]
        at = slice(width * i, width * (i + 1))
        rows = slice(share * 3, share * 4)
        term = dot3(high, low, mid_high[rows, :], mid_low[rows, :])
        out_ref[:, at] = (total_ref[:, at] + term) * scale[:, at]


SMEM = pl.BlockSpec(memory_space=pltpu.SMEM)
VMEM = pl.BlockSpec(memory_space=pltpu.VMEM)


def call(kernel, name, outs, inputs, flops=0, scratch=()):
    shapes = [(jax.ShapeDtypeStruct if name == "finish" else pltpu.VMEM)(shape, kind) for shape, kind in outs]
    moved = sum(x.size * x.dtype.itemsize for x in inputs) + sum(math.prod(s) * jnp.dtype(k).itemsize for s, k in outs)
    return pl.pallas_call(
        kernel,
        name=name,
        out_shape=shapes,
        in_specs=[SMEM if x.size == 4 else VMEM for x in inputs],
        out_specs=[VMEM] * len(shapes),
        scratch_shapes=list(scratch),
        cost_estimate=pl.CostEstimate(flops=flops, bytes_accessed=moved, transcendentals=0),
        compiler_params=pltpu.CompilerParams(vmem_limit_bytes=SOME_VMEM),
    )(*inputs)


def body(vectors_in, poles_one, roots_one, order_one, deflate_one, poles_two, roots_two, order_two, deflate_two):
    row_total = lax.axis_size("row")
    assert lax.axis_size("col") == 4
    row_place = lax.axis_index("row")
    col_place = lax.axis_index("col")
    local_rows, share = vectors_in.shape
    leaf = 4 * share
    width_one = 2 * leaf
    width_two = 4 * leaf
    columns = width_two // 4
    per_leaf = row_total // 4
    leaf_number = row_place // per_leaf
    pair = leaf_number // 2
    side = leaf_number % 2
    place = jnp.stack([pair, side, col_place, row_place]).astype(jnp.int32)
    roots_two, order_two, poles_two, deflate_two = (
        a.reshape(1, width_two) for a in (roots_two, order_two, poles_two, deflate_two)
    )

    def along_col(x, moves):
        return lax.ppermute(x, "col", moves)

    far = along_col(vectors_in, [(0, 2), (1, 3), (2, 0), (3, 1)])
    near = along_col(vectors_in, [(0, 1), (1, 0), (2, 3), (3, 2)])

    first_row, last_row = vectors_in[0:1], vectors_in[local_rows - 1 :]
    start = 2 * pair * per_leaf
    edges = jnp.concatenate(
        [
            jnp.where(row_place == start + per_leaf - 1, last_row, 0.0),
            jnp.where(row_place == start + per_leaf, first_row, 0.0),
            jnp.where(row_place == 2 * per_leaf - 1, last_row, jnp.where(row_place == 2 * per_leaf, first_row, 0.0)),
            jnp.zeros((5, share), F32),
        ],
        axis=0,
    )
    step = 1
    while step < 2 * per_leaf:
        edges = edges + lax.ppermute(edges, "row", [(i, i ^ step) for i in range(row_total)])
        step *= 2

    blocks = width_one // LANES
    one_cols, two_cols = call(
        perm_kernel, "orders", [((LANES, 2 * blocks), F32)] * 2,
        [place, order_one, poles_one, deflate_one, order_two, poles_two, deflate_two],
    )
    one_high, one_low = call(
        table_one_kernel, "table_one", [((leaf, width_one), BF16)] * 2,
        [place, one_cols, roots_one, deflate_one], flops=10 * leaf * width_one,
    )
    (table_two,) = call(
        table_two_kernel, "table_two", [((width_one, columns), F32)],
        [place, two_cols, roots_two, deflate_two], flops=10 * width_one * columns,
    )
    (sums,) = call(
        norm_one_kernel, "norm_one", [((4, width_one), F32)],
        [place, edges, one_cols, roots_one, deflate_one], flops=10 * 2 * share * width_one,
        scratch=[pltpu.VMEM((share // LANES, LANES, 8), F32)],
    )
    sums_moved = [along_col(sums, [(i, i ^ k) for i in range(4)]) for k in (1, 2, 3)]
    (weights,) = call(
        weight_kernel, "weights", [((LANES, 2 * blocks + blocks // 2), F32)],
        [place, sums, *sums_moved, deflate_one, one_cols, two_cols],
    )
    weights, far = lax.optimization_barrier((weights, far))
    halves = []
    squares = []
    width = columns // 2
    for i in range(2):
        mid_high, mid_low, part = call(
            functools.partial(mid_kernel, i), "mid", [((leaf, width), BF16)] * 2 + [((1, width), F32)],
            [weights, one_high, one_low, table_two],
            flops=6 * leaf * width_one * width,
            scratch=[pltpu.VMEM((width_one, width), BF16)] * 2,
        )
        halves += [mid_high, mid_low]
        squares.append(part)
    half_row = row_total // 2
    squares_far = lax.ppermute(
        jnp.concatenate(squares, axis=1), "row", [(i, (i + half_row) % row_total) for i in range(row_total)]
    )
    third = along_col(far, [(1, 0), (2, 3)])
    fourth = along_col(vectors_in, [(1, 2), (2, 1)])
    (total,) = call(
        functools.partial(apply_kernel, 3), "apply", [((local_rows, columns), F32)],
        [vectors_in, near, far, *halves], flops=6 * local_rows * 3 * share * columns,
    )
    (merged,) = call(
        finish_kernel, "finish", [((local_rows, columns), F32)],
        [place, total, third, fourth, *squares, squares_far, deflate_two, *halves],
        flops=6 * local_rows * share * columns,
    )
    return merged


def solution(mesh):
    placed = (P("row", "col"), P(), P(), P(), P(), P(), P(), P(), P())
    return jax.shard_map(body, mesh=mesh, in_specs=placed, out_specs=P("row", "col"), check_vma=False)
```

```python
import functools
import math

import jax
import jax.numpy as jnp
from jax import lax
from jax.experimental import pallas as pl
from jax.experimental.pallas import tpu as pltpu
from jax.sharding import PartitionSpec as P

F32 = jnp.float32
BF16 = jnp.bfloat16
LANES = 128
SOME_VMEM = 14 * 1024 * 1024
ROWS, WIDTH = 32, 512
PIECES = (1, 2)
WEIGHTS = {"orders": 100, "table_one": 100, "table_two": 100, "norm_one": 100, "apply": 0.001, "finish": 0.001}


def split(x):
    high = x.astype(BF16)
    return high, (x - high.astype(F32)).astype(BF16)


def dot3(a_high, a_low, b_high, b_low):
    dot = functools.partial(jnp.dot, preferred_element_type=F32)
    return dot(a_high, b_high) + dot(a_low, b_high) + dot(a_high, b_low)


def as_columns(row):
    count = row.shape[1] // LANES
    stacked = jnp.concatenate([row[:, LANES * b : LANES * (b + 1)] for b in range(count)], axis=0)
    return stacked.T


def permuted(order, low_bits, wanted, values):
    at_high = order >> 7 == wanted
    at_low = ((order & 127) == low_bits).astype(BF16)
    rows = jnp.concatenate([jnp.where(at_high, v, 0.0).astype(BF16) for v in values], axis=0)
    out = lax.dot_general(rows, at_low, (((1,), (1,)), ((), ())), preferred_element_type=F32)
    count = wanted.shape[0]
    return [out[count * i : count * (i + 1)] for i in range(len(values))]


def place_tables(order, poles, flags, wanted):
    span = order.shape[1]
    low_bits = lax.broadcasted_iota(jnp.int32, (LANES, span), 0)
    index = lax.broadcasted_iota(jnp.int32, (1, span), 1)
    first = poles.astype(BF16).astype(F32)
    second = (poles - first).astype(BF16).astype(F32)
    third = poles - first - second
    values = [first, second, third, (index >> 6).astype(F32), (index & 63).astype(F32), flags.astype(F32)]
    one, two, three, upper, lower, flag = permuted(order, low_bits, wanted, values)
    gone = flag > 0.5
    pole = jnp.where(gone, jnp.inf, one + two + three)
    target = jnp.where(gone, upper * 64.0 + lower, -1.0)
    return pole, target


def perm_kernel(place, *refs):
    given, outs, (held, arrived) = refs[:8], refs[8:14], (refs[14:22], refs[22])
    one_out, two_out, roots_one_out, flags_one_out, roots_two_out, flags_two_out = outs
    copies = [pltpu.make_async_copy(x, y, arrived.at[i]) for i, (x, y) in enumerate(zip(given, held))]
    for copy in copies:
        copy.start()
    for copy in copies:
        copy.wait()
    poles_one, roots_one, order_one, flags_one, poles_two, roots_two, order_two, flags_two = held
    pair, side, piece, core = place[0], place[1], place[2], place[3]
    blocks = order_one.shape[1] // LANES
    spot = lax.broadcasted_iota(jnp.int32, (blocks, 1), 0)
    half = blocks // 2
    per = half // 4
    late = spot - half // 2
    wanted_one = jnp.where(late < 0, side, 1 - side) * half
    wanted_one += (((spot % (half // 2)) // per) ^ piece ^ (2 * core)) * per + spot % per
    wanted_one = jnp.where(spot < half, wanted_one, -1)
    at = pl.ds(pair, 1)
    flags = flags_one[at, :]
    flags_one_out[...] = flags
    roots_one_out[...] = jnp.where(flags > 0, -jnp.inf, roots_one[at, :])
    pole, target = place_tables(order_one[at, :], poles_one[at, :], flags, wanted_one)
    one_out[...] = jnp.concatenate([pole, target], axis=0).T
    columns = roots_two_out.shape[1]
    lanes = pl.ds(pl.multiple_of(piece * columns, LANES), columns)
    flags = flags_two[:, lanes]
    flags_two_out[...] = flags
    roots_two_out[...] = jnp.where(flags > 0, -jnp.inf, roots_two[:, lanes])
    pole, target = place_tables(order_two[...], poles_two[...], flags_two[...], spot + pair * blocks)
    two_out[...] = jnp.concatenate([pole, target], axis=0).T


def inverse_gap(pole, target, roots, index):
    gap = pltpu.reciprocal(pole - roots, approx=True)
    return jnp.where(target == index, 1.0, gap)


def over_tiles(height, width, tile):
    for first in range(0, width, WIDTH):
        lanes = slice(first, first + WIDTH)
        for b in range(height // LANES):

            def step(i, _, b=b, lanes=lanes):
                near = pl.multiple_of(i * ROWS, ROWS)
                tile(b, pl.ds(near, ROWS), pl.ds(pl.multiple_of(b * LANES + near, ROWS), ROWS), lanes)
                return 0

            lax.fori_loop(0, LANES // ROWS, step, 0, unroll=LANES // ROWS)


def table_one_kernel(cols_ref, roots_ref, high_ref, low_ref):
    roots = roots_ref[...]
    index = lax.broadcasted_iota(jnp.int32, roots.shape, 1).astype(F32)
    blocks = cols_ref.shape[1] // 2

    def tile(b, near, rows, lanes):
        pole, target = cols_ref[near, b : b + 1], cols_ref[near, blocks + b : blocks + b + 1]
        high_ref[rows, lanes], low_ref[rows, lanes] = split(inverse_gap(pole, target, roots[:, lanes], index[:, lanes]))

    over_tiles(*high_ref.shape, tile)


def table_two_kernel(place, cols_ref, roots_ref, out_ref):
    roots = roots_ref[...]
    index = (lax.broadcasted_iota(jnp.int32, roots.shape, 1) + place[2] * out_ref.shape[1]).astype(F32)
    blocks = cols_ref.shape[1] // 2

    def tile(b, near, rows, lanes):
        pole, target = cols_ref[near, b : b + 1], cols_ref[near, blocks + b : blocks + b + 1]
        out_ref[rows, lanes] = inverse_gap(pole, target, roots[:, lanes], index[:, lanes])

    over_tiles(*out_ref.shape, tile)


def add_rows(total, x):
    for i in range(0, x.shape[0], 8):
        total = total + x[i : i + 8]
    return total


def norm_one_kernel(place, edge_ref, cols_ref, roots_ref, out_ref, edge_cols):
    pair, side, core = place[0], place[1], place[3]
    roots = roots_ref[...]
    width = roots.shape[1]
    index = lax.broadcasted_iota(jnp.int32, roots.shape, 1).astype(F32)
    blocks = cols_ref.shape[1] // 2
    share = edge_ref.shape[1] // 2
    edges = edge_ref[:, pl.ds(pl.multiple_of(core * share, LANES), share)]
    own = jnp.where(side == 0, edges[0:1], edges[1:2])
    other = jnp.where(side == 0, edges[1:2], edges[0:1])
    own_edge = jnp.where(side == 1 - pair, edges[2:3], 0.0)
    other_edge = jnp.where(side == 1 - pair, 0.0, edges[2:3])
    pad = jnp.zeros((4, share), F32)
    rows_all = jnp.concatenate([own, other, own_edge, other_edge, pad], axis=0)
    for b in range(share // LANES):
        edge_cols[b] = rows_all[:, LANES * b : LANES * (b + 1)].T
    for first in range(0, width, WIDTH):
        lanes = slice(first, first + WIDTH)
        carry = (jnp.zeros((8, WIDTH), F32), jnp.zeros((8, WIDTH), F32))
        for part in range(2):
            for b in range(share // LANES):
                block = part * (share // LANES) + b

                def step(i, carry, part=part, b=b, block=block, lanes=lanes):
                    rows = pl.ds(pl.multiple_of(i * ROWS, ROWS), ROWS)
                    target = cols_ref[rows, blocks + block : blocks + block + 1]
                    gap = pltpu.reciprocal(cols_ref[rows, block : block + 1] - roots[:, lanes], approx=True)
                    z = edge_cols[b, rows, part : part + 1]
                    edge = edge_cols[b, rows, 2 + part : 3 + part]
                    scaled = z * gap
                    weighed = edge * jnp.where(target == index[:, lanes], 1.0, scaled)
                    return add_rows(carry[0], scaled * scaled), add_rows(carry[1], weighed)

                carry = lax.fori_loop(0, LANES // ROWS, step, carry, unroll=LANES // ROWS)
        out_ref[0:1, lanes] = jnp.sum(carry[0], axis=0, keepdims=True)
        out_ref[1:2, lanes] = jnp.sum(carry[1], axis=0, keepdims=True)


def weight_kernel(place, here, there, edge_ref, flags_ref, one_cols, two_cols, out_ref):
    squares = here[0:1, :] + there[0:1, :]
    edge = here[1:2, :] + there[1:2, :]
    gone = flags_ref[...] > 0
    scale = as_columns(jnp.where(gone, 1.0, lax.rsqrt(squares + 1e-06)))
    blocks = two_cols.shape[1] // 2
    z_two = as_columns(edge) * scale
    row_gone = two_cols[:, blocks:] >= 0.0
    out_ref[:, 0:blocks] = scale * jnp.where(row_gone, 1.0, z_two)
    out_ref[:, blocks : 2 * blocks] = jnp.where(row_gone, 0.0, z_two)
    share = edge_ref.shape[1] // 2
    edges = edge_ref[:, pl.ds(pl.multiple_of(place[3] * share, LANES), share)]
    z_one = as_columns(jnp.where(place[1] == 0, edges[0:1], edges[1:2]))
    count = z_one.shape[1]
    row_gone = one_cols[:, blocks : blocks + count] >= 0.0
    out_ref[:, 2 * blocks : 2 * blocks + count] = jnp.where(row_gone, 1.0, z_one)


def scale_kernel(weights, two_ref, b_high, b_low, squares_ref):
    depth, columns = b_high.shape
    blocks = depth // LANES
    for first in range(0, columns, WIDTH):
        lanes = slice(first, first + WIDTH)
        squares = jnp.zeros((8, WIDTH), F32)
        for b in range(blocks):

            def step(i, squares, b=b, lanes=lanes):
                rows = pl.ds(pl.multiple_of(i * ROWS, ROWS), ROWS)
                to = pl.ds(pl.multiple_of(b * LANES + i * ROWS, ROWS), ROWS)
                table = two_ref[to, lanes]
                b_high[to, lanes], b_low[to, lanes] = split(table * weights[rows, b : b + 1])
                scaled = table * weights[rows, blocks + b : blocks + b + 1]
                return add_rows(squares, scaled * scaled)

            squares = lax.fori_loop(0, LANES // ROWS, step, squares, unroll=LANES // ROWS)
        squares_ref[:, lanes] = jnp.sum(squares, axis=0, keepdims=True)


def mid_kernel(part, weights, high_ref, low_ref, b_high, b_low, *outs):
    piece, columns = outs[0].shape
    height = piece * len(outs)
    blocks = b_high.shape[0] // LANES
    rows = slice(height * part, height * (part + 1))
    for first in range(0, columns, WIDTH):
        lanes = slice(first, first + WIDTH)
        mid = dot3(high_ref[rows, :], low_ref[rows, :], b_high[:, lanes], b_low[:, lanes])
        for i, out_ref in enumerate(outs):
            for begin in range(0, piece, LANES):
                count = min(LANES, piece)
                b, inner = divmod(piece * i + begin, LANES)
                at = 2 * blocks + part * (height // LANES) + b
                scale = weights[inner : inner + count, at : at + 1]
                out_ref[begin : begin + count, lanes] = mid[piece * i + begin : piece * i + begin + count] * scale


def apply_kernel(place, own_mid, other_mid, mine, far, out_ref):
    first = place[3] == 0
    own = split(jnp.where(first, mine[...], far[...]))
    other = split(jnp.where(first, far[...], mine[...]))
    for at in range(0, out_ref.shape[1], WIDTH):
        lanes = slice(at, at + WIDTH)
        out_ref[:, lanes] = dot3(*own, *split(own_mid[:, lanes])) + dot3(*other, *split(other_mid[:, lanes]))


def finish_kernel(place, near_ref, last_end, last_middle, total_ref, squares, squares_far, flags_ref, *refs):
    count = len(refs) // 2 - 1
    own_late, other_late, (out_ref, done, left) = refs[:count], refs[count : 2 * count], refs[2 * count :]
    scale = jnp.where(flags_ref[...] > 0, 1.0, lax.rsqrt(squares[...] + squares_far[...] + 1e-06))
    first = place[3] == 0
    near, last = near_ref[...], last_end[...] + last_middle[...]
    own = split(jnp.where(first, near, last))
    other = split(jnp.where(first, last, near))
    copies = []
    for i, at in enumerate(range(0, out_ref.shape[1], WIDTH)):
        lanes = slice(at, at + WIDTH)
        own_mid = jnp.concatenate([x[:, lanes] for x in own_late], axis=0)
        other_mid = jnp.concatenate([x[:, lanes] for x in other_late], axis=0)
        term = dot3(*own, *split(own_mid)) + dot3(*other, *split(other_mid))
        done[:, lanes] = (total_ref[:, lanes] + term) * scale[:, lanes]
        copies.append(pltpu.make_async_copy(done.at[:, lanes], out_ref.at[:, lanes], left.at[i]))
        copies[-1].start()
    for copy in copies:
        copy.wait()


SMEM = pl.BlockSpec(memory_space=pltpu.SMEM)
VMEM = pl.BlockSpec(memory_space=pltpu.VMEM)
HBM = pl.BlockSpec(memory_space=pltpu.HBM)


def call(kernel, name, outs, inputs, flops=0, scratch=()):
    shapes = [(jax.ShapeDtypeStruct if name == "finish" else pltpu.VMEM)(shape, kind) for shape, kind in outs]
    weight = WEIGHTS.get(name, 1)
    moved = sum(x.size * x.dtype.itemsize for x in inputs) + sum(math.prod(s) * jnp.dtype(k).itemsize for s, k in outs)
    return pl.pallas_call(
        kernel,
        name=name,
        out_shape=shapes,
        in_specs=[SMEM if x.size == 4 else HBM if name == "orders" else VMEM for x in inputs],
        out_specs=[HBM if name == "finish" else VMEM] * len(shapes),
        scratch_shapes=list(scratch),
        cost_estimate=pl.CostEstimate(flops=int(flops * weight), bytes_accessed=int(moved * weight), transcendentals=0),
        compiler_params=pltpu.CompilerParams(vmem_limit_bytes=SOME_VMEM),
    )(*inputs)


def body(vectors_in, poles_one, roots_one, order_one, deflate_one, poles_two, roots_two, order_two, deflate_two):
    row_total = lax.axis_size("row")
    assert lax.axis_size("col") == 4
    row_place = lax.axis_index("row")
    col_place = lax.axis_index("col")
    local_rows, share = vectors_in.shape
    leaf = 4 * share
    width_one = 2 * leaf
    width_two = 4 * leaf
    columns = width_two // 4
    per_leaf = row_total // 4
    assert per_leaf % 2 == 0
    leaf_number = row_place // per_leaf
    pair = leaf_number // 2
    side = leaf_number % 2
    place = jnp.stack([pair, side, col_place, row_place % 2]).astype(jnp.int32)
    roots_two, order_two, poles_two, deflate_two = (
        a.reshape(1, width_two) for a in (roots_two, order_two, poles_two, deflate_two)
    )

    def along_col(x, moves):
        return lax.ppermute(x, "col", moves)

    rows = jnp.concatenate([vectors_in[0:1], vectors_in[local_rows - 1 :]], axis=0)
    rows = jnp.concatenate([rows] + [along_col(rows, [(i, i ^ k) for i in range(4)]) for k in (1, 2, 3)], axis=1)
    far = along_col(vectors_in, [(0, 2), (1, 3), (2, 0), (3, 1)])
    near = along_col(vectors_in, [(0, 1), (1, 0), (2, 3), (3, 2)])

    first_row, last_row = rows[0:1], rows[1:2]
    start = 2 * pair * per_leaf
    edges = jnp.concatenate(
        [
            jnp.where(row_place == start + per_leaf - 1, last_row, 0.0),
            jnp.where(row_place == start + per_leaf, first_row, 0.0),
            jnp.where(row_place == 2 * per_leaf - 1, last_row, jnp.where(row_place == 2 * per_leaf, first_row, 0.0)),
            jnp.zeros((5, leaf), F32),
        ],
        axis=0,
    )
    step = 1
    while step < 2 * per_leaf:
        edges = edges + lax.ppermute(edges, "row", [(i, i ^ step) for i in range(row_total)])
        step *= 2

    blocks = width_one // LANES
    raw = [poles_one, roots_one, order_one, deflate_one, poles_two, roots_two, order_two, deflate_two]
    raw = [pltpu.with_memory_space_constraint(x, pltpu.HBM) for x in raw]
    one_cols, two_cols, roots_one, flags_one, roots_two, flags_two = call(
        perm_kernel, "orders",
        [((LANES, 2 * blocks), F32)] * 2
        + [((1, width_one), F32), ((1, width_one), jnp.int32), ((1, columns), F32), ((1, columns), jnp.int32)],
        [place, *raw],
        scratch=[pltpu.VMEM(x.shape, x.dtype) for x in raw] + [pltpu.SemaphoreType.DMA((len(raw),))],
    )
    (sums,) = call(
        norm_one_kernel, "norm_one", [((2, width_one), F32)],
        [place, edges, one_cols, roots_one], flops=10 * leaf * width_one,
        scratch=[pltpu.VMEM((2 * share // LANES, LANES, 8), F32)],
    )
    sums_there = lax.ppermute(sums, "row", [(i, i ^ 1) for i in range(row_total)])
    one_high, one_low = call(
        table_one_kernel, "table_one", [((leaf // 2, width_one), BF16)] * 2,
        [one_cols, roots_one], flops=10 * leaf * width_one,
    )
    (table_two,) = call(
        table_two_kernel, "table_two", [((width_one, columns), F32)],
        [place, two_cols, roots_two], flops=10 * width_one * columns,
    )
    (weights,) = call(
        weight_kernel, "weights", [((LANES, 2 * blocks + leaf // 2 // LANES), F32)],
        [place, sums, sums_there, edges, flags_one, one_cols, two_cols],
    )
    b_high, b_low, squares = call(
        scale_kernel, "scale", [((width_one, columns), BF16)] * 2 + [((1, columns), F32)],
        [weights, table_two], flops=10 * width_one * columns,
    )
    half_row = row_total // 2
    squares_far = lax.ppermute(squares, "row", [(i, (i + half_row) % row_total) for i in range(row_total)])
    own_mids, other_mids = [], []
    for part in range(2):
        pieces = PIECES[part]
        own = call(
            functools.partial(mid_kernel, part), "mid", [((share // pieces, columns), F32)] * pieces,
            [weights, one_high, one_low, b_high, b_low], flops=6 * share * width_one * columns,
        )
        own_mids.append(own)
        if part == 0:
            b_high, near, far, from_middle = lax.optimization_barrier((b_high, near, far, vectors_in))
            last_end = along_col(far, [(1, 0), (2, 3)])
            last_middle = along_col(from_middle, [(1, 2), (2, 1)])
        other_mids.append([lax.ppermute(x, "row", [(i, i ^ 1) for i in range(row_total)]) for x in own])
    (total,) = call(
        apply_kernel, "apply", [((local_rows, columns), F32)],
        [place, *own_mids[0], *other_mids[0], vectors_in, far], flops=6 * local_rows * 2 * share * columns,
    )
    token, last_end, last_middle, total = lax.optimization_barrier((squares[:, :LANES], last_end, last_middle, total))
    token = lax.ppermute(token, "row", [(i, i ^ 1) for i in range(row_total)])
    total, token = lax.optimization_barrier((total, token))
    (merged,) = call(
        finish_kernel, "finish", [((local_rows, columns), F32)],
        [place, near, last_end, last_middle, total, squares, squares_far, flags_two, *own_mids[1], *other_mids[1]],
        flops=6 * local_rows * 2 * share * columns,
        scratch=[pltpu.VMEM((local_rows, columns), F32), pltpu.SemaphoreType.DMA((columns // WIDTH,))],
    )
    return merged


def solution(mesh):
    placed = (P("row", "col"), P(), P(), P(), P(), P(), P(), P(), P())
    return jax.shard_map(body, mesh=mesh, in_specs=placed, out_specs=P("row", "col"), check_vma=False)
```

```python
import functools
import math

import jax
import jax.numpy as jnp
from jax import lax
from jax.experimental import pallas as pl
from jax.experimental.pallas import tpu as pltpu
from jax.sharding import PartitionSpec as P

F32 = jnp.float32
BF16 = jnp.bfloat16
LANES = 128
SOME_VMEM = 14 * 1024 * 1024
ROWS, WIDTH = 32, 512
PIECES = (1, 2)
WEIGHTS = {"orders": 100, "table_one": 100, "table_two": 100, "norm_one": 100, "apply": 0.001, "finish": 0.001}


def split(x):
    high = x.astype(BF16)
    return high, (x - high.astype(F32)).astype(BF16)


def dot3(a_high, a_low, b_high, b_low):
    dot = functools.partial(jnp.dot, preferred_element_type=F32)
    return dot(a_high, b_high) + dot(a_low, b_high) + dot(a_high, b_low)


def as_columns(row):
    count = row.shape[1] // LANES
    stacked = jnp.concatenate([row[:, LANES * b : LANES * (b + 1)] for b in range(count)], axis=0)
    return stacked.T


def permuted(order, low_bits, wanted, values):
    at_high = order >> 7 == wanted
    at_low = ((order & 127) == low_bits).astype(BF16)
    rows = jnp.concatenate([jnp.where(at_high, v, 0.0).astype(BF16) for v in values], axis=0)
    out = lax.dot_general(rows, at_low, (((1,), (1,)), ((), ())), preferred_element_type=F32)
    count = wanted.shape[0]
    return [out[count * i : count * (i + 1)] for i in range(len(values))]


def place_tables(order, poles, flags, wanted):
    span = order.shape[1]
    low_bits = lax.broadcasted_iota(jnp.int32, (LANES, span), 0)
    index = lax.broadcasted_iota(jnp.int32, (1, span), 1)
    first = poles.astype(BF16).astype(F32)
    second = (poles - first).astype(BF16).astype(F32)
    third = poles - first - second
    values = [first, second, third, (index >> 6).astype(F32), (index & 63).astype(F32), flags.astype(F32)]
    one, two, three, upper, lower, flag = permuted(order, low_bits, wanted, values)
    gone = flag > 0.5
    pole = jnp.where(gone, jnp.inf, one + two + three)
    target = jnp.where(gone, upper * 64.0 + lower, -1.0)
    return pole, target


def perm_kernel(place, *refs):
    given, outs, (held, arrived) = refs[:8], refs[8:14], (refs[14:22], refs[22])
    one_out, two_out, roots_one_out, flags_one_out, roots_two_out, flags_two_out = outs
    copies = [pltpu.make_async_copy(x, y, arrived.at[i]) for i, (x, y) in enumerate(zip(given, held))]
    for copy in copies:
        copy.start()
    for copy in copies:
        copy.wait()
    poles_one, roots_one, order_one, flags_one, poles_two, roots_two, order_two, flags_two = held
    pair, side, piece, core = place[0], place[1], place[2], place[3]
    blocks = order_one.shape[1] // LANES
    spot = lax.broadcasted_iota(jnp.int32, (blocks, 1), 0)
    half = blocks // 2
    per = half // 4
    late = spot - half // 2
    wanted_one = jnp.where(late < 0, side, 1 - side) * half
    wanted_one += (((spot % (half // 2)) // per) ^ piece ^ (2 * core)) * per + spot % per
    wanted_one = jnp.where(spot < half, wanted_one, -1)
    at = pl.ds(pair, 1)
    flags = flags_one[at, :]
    flags_one_out[...] = flags
    roots_one_out[...] = jnp.where(flags > 0, -jnp.inf, roots_one[at, :])
    pole, target = place_tables(order_one[at, :], poles_one[at, :], flags, wanted_one)
    one_out[...] = jnp.concatenate([pole, target], axis=0).T
    columns = roots_two_out.shape[1]
    lanes = pl.ds(pl.multiple_of(piece * columns, LANES), columns)
    flags = flags_two[:, lanes]
    flags_two_out[...] = flags
    roots_two_out[...] = jnp.where(flags > 0, -jnp.inf, roots_two[:, lanes])
    pole, target = place_tables(order_two[...], poles_two[...], flags_two[...], spot + pair * blocks)
    two_out[...] = jnp.concatenate([pole, target], axis=0).T


def inverse_gap(pole, target, roots, index):
    gap = pltpu.reciprocal(pole - roots, approx=True)
    return jnp.where(target == index, 1.0, gap)


def over_tiles(height, width, tile):
    for first in range(0, width, WIDTH):
        lanes = slice(first, first + WIDTH)
        for b in range(height // LANES):

            def step(i, _, b=b, lanes=lanes):
                near = pl.multiple_of(i * ROWS, ROWS)
                tile(b, pl.ds(near, ROWS), pl.ds(pl.multiple_of(b * LANES + near, ROWS), ROWS), lanes)
                return 0

            lax.fori_loop(0, LANES // ROWS, step, 0, unroll=LANES // ROWS)


def table_one_kernel(cols_ref, roots_ref, high_ref, low_ref):
    roots = roots_ref[...]
    index = lax.broadcasted_iota(jnp.int32, roots.shape, 1).astype(F32)
    blocks = cols_ref.shape[1] // 2

    def tile(b, near, rows, lanes):
        pole, target = cols_ref[near, b : b + 1], cols_ref[near, blocks + b : blocks + b + 1]
        high_ref[rows, lanes], low_ref[rows, lanes] = split(inverse_gap(pole, target, roots[:, lanes], index[:, lanes]))

    over_tiles(*high_ref.shape, tile)


def table_two_kernel(place, cols_ref, roots_ref, out_ref):
    roots = roots_ref[...]
    index = (lax.broadcasted_iota(jnp.int32, roots.shape, 1) + place[2] * out_ref.shape[1]).astype(F32)
    blocks = cols_ref.shape[1] // 2

    def tile(b, near, rows, lanes):
        pole, target = cols_ref[near, b : b + 1], cols_ref[near, blocks + b : blocks + b + 1]
        out_ref[rows, lanes] = inverse_gap(pole, target, roots[:, lanes], index[:, lanes])

    over_tiles(*out_ref.shape, tile)


def add_rows(total, x):
    for i in range(0, x.shape[0], 8):
        total = total + x[i : i + 8]
    return total


def norm_one_kernel(place, edge_ref, cols_ref, roots_ref, out_ref, edge_cols):
    pair, side, core = place[0], place[1], place[3]
    roots = roots_ref[...]
    width = roots.shape[1]
    index = lax.broadcasted_iota(jnp.int32, roots.shape, 1).astype(F32)
    blocks = cols_ref.shape[1] // 2
    share = edge_ref.shape[1] // 2
    edges = edge_ref[:, pl.ds(pl.multiple_of(core * share, LANES), share)]
    own = jnp.where(side == 0, edges[0:1], edges[1:2])
    other = jnp.where(side == 0, edges[1:2], edges[0:1])
    own_edge = jnp.where(side == 1 - pair, edges[2:3], 0.0)
    other_edge = jnp.where(side == 1 - pair, 0.0, edges[2:3])
    pad = jnp.zeros((4, share), F32)
    rows_all = jnp.concatenate([own, other, own_edge, other_edge, pad], axis=0)
    for b in range(share // LANES):
        edge_cols[b] = rows_all[:, LANES * b : LANES * (b + 1)].T
    for first in range(0, width, WIDTH):
        lanes = slice(first, first + WIDTH)
        carry = (jnp.zeros((8, WIDTH), F32), jnp.zeros((8, WIDTH), F32))
        for part in range(2):
            for b in range(share // LANES):
                block = part * (share // LANES) + b

                def step(i, carry, part=part, b=b, block=block, lanes=lanes):
                    rows = pl.ds(pl.multiple_of(i * ROWS, ROWS), ROWS)
                    target = cols_ref[rows, blocks + block : blocks + block + 1]
                    gap = pltpu.reciprocal(cols_ref[rows, block : block + 1] - roots[:, lanes], approx=True)
                    z = edge_cols[b, rows, part : part + 1]
                    edge = edge_cols[b, rows, 2 + part : 3 + part]
                    scaled = z * gap
                    weighed = edge * jnp.where(target == index[:, lanes], 1.0, scaled)
                    return add_rows(carry[0], scaled * scaled), add_rows(carry[1], weighed)

                carry = lax.fori_loop(0, LANES // ROWS, step, carry, unroll=LANES // ROWS)
        out_ref[0:1, lanes] = jnp.sum(carry[0], axis=0, keepdims=True)
        out_ref[1:2, lanes] = jnp.sum(carry[1], axis=0, keepdims=True)


def weight_kernel(place, here, there, edge_ref, flags_ref, one_cols, two_cols, out_ref):
    squares = here[0:1, :] + there[0:1, :]
    edge = here[1:2, :] + there[1:2, :]
    gone = flags_ref[...] > 0
    scale = as_columns(jnp.where(gone, 1.0, lax.rsqrt(squares + 1e-06)))
    blocks = two_cols.shape[1] // 2
    z_two = as_columns(edge) * scale
    row_gone = two_cols[:, blocks:] >= 0.0
    out_ref[:, 0:blocks] = scale * jnp.where(row_gone, 1.0, z_two)
    out_ref[:, blocks : 2 * blocks] = jnp.where(row_gone, 0.0, z_two)
    share = edge_ref.shape[1] // 2
    edges = edge_ref[:, pl.ds(pl.multiple_of(place[3] * share, LANES), share)]
    z_one = as_columns(jnp.where(place[1] == 0, edges[0:1], edges[1:2]))
    count = z_one.shape[1]
    row_gone = one_cols[:, blocks : blocks + count] >= 0.0
    out_ref[:, 2 * blocks : 2 * blocks + count] = jnp.where(row_gone, 1.0, z_one)


def scale_kernel(weights, two_ref, b_high, b_low, squares_ref):
    depth, columns = b_high.shape
    blocks = depth // LANES
    for first in range(0, columns, WIDTH):
        lanes = slice(first, first + WIDTH)
        squares = jnp.zeros((8, WIDTH), F32)
        for b in range(blocks):

            def step(i, squares, b=b, lanes=lanes):
                rows = pl.ds(pl.multiple_of(i * ROWS, ROWS), ROWS)
                to = pl.ds(pl.multiple_of(b * LANES + i * ROWS, ROWS), ROWS)
                table = two_ref[to, lanes]
                b_high[to, lanes], b_low[to, lanes] = split(table * weights[rows, b : b + 1])
                scaled = table * weights[rows, blocks + b : blocks + b + 1]
                return add_rows(squares, scaled * scaled)

            squares = lax.fori_loop(0, LANES // ROWS, step, squares, unroll=LANES // ROWS)
        squares_ref[:, lanes] = jnp.sum(squares, axis=0, keepdims=True)


def mid_kernel(part, weights, high_ref, low_ref, b_high, b_low, *outs):
    piece, columns = outs[0].shape
    height = piece * len(outs)
    blocks = b_high.shape[0] // LANES
    rows = slice(height * part, height * (part + 1))
    for first in range(0, columns, WIDTH):
        lanes = slice(first, first + WIDTH)
        mid = dot3(high_ref[rows, :], low_ref[rows, :], b_high[:, lanes], b_low[:, lanes])
        for i, out_ref in enumerate(outs):
            for begin in range(0, piece, LANES):
                count = min(LANES, piece)
                b, inner = divmod(piece * i + begin, LANES)
                at = 2 * blocks + part * (height // LANES) + b
                scale = weights[inner : inner + count, at : at + 1]
                out_ref[begin : begin + count, lanes] = mid[piece * i + begin : piece * i + begin + count] * scale


def apply_kernel(place, own_mid, other_mid, mine, far, out_ref):
    first = place[3] == 0
    own = split(jnp.where(first, mine[...], far[...]))
    other = split(jnp.where(first, far[...], mine[...]))
    for at in range(0, out_ref.shape[1], WIDTH):
        lanes = slice(at, at + WIDTH)
        out_ref[:, lanes] = dot3(*own, *split(own_mid[:, lanes])) + dot3(*other, *split(other_mid[:, lanes]))


def finish_kernel(place, near_ref, last_end, last_middle, total_ref, squares, squares_far, flags_ref, *refs):
    count = len(refs) // 2 - 1
    own_late, other_late, (out_ref, done, left) = refs[:count], refs[count : 2 * count], refs[2 * count :]
    scale = jnp.where(flags_ref[...] > 0, 1.0, lax.rsqrt(squares[...] + squares_far[...] + 1e-06))
    first = place[3] == 0
    near, last = near_ref[...], last_end[...] + last_middle[...]
    own, other = jnp.where(first, near, last), jnp.where(first, last, near)
    own_mid = split(jnp.concatenate([x[...] for x in own_late], axis=0))
    other_mid = split(jnp.concatenate([x[...] for x in other_late], axis=0))
    copies = []
    height = out_ref.shape[0] // left.shape[0]
    for i in range(left.shape[0]):
        rows = slice(height * i, height * (i + 1))
        term = dot3(*split(own[rows]), *own_mid) + dot3(*split(other[rows]), *other_mid)
        done[rows, :] = (total_ref[rows, :] + term) * scale
        copies.append(pltpu.make_async_copy(done.at[rows, :], out_ref.at[rows, :], left.at[i]))
        copies[-1].start()
    for copy in copies:
        copy.wait()


SMEM = pl.BlockSpec(memory_space=pltpu.SMEM)
VMEM = pl.BlockSpec(memory_space=pltpu.VMEM)
HBM = pl.BlockSpec(memory_space=pltpu.HBM)


def coordinates():
    per_leaf = lax.axis_size("row") // 4
    row = lax.axis_index("row")
    leaf = lax.div(row, jnp.int32(per_leaf))
    return lax.div(leaf, jnp.int32(2)), lax.rem(leaf, jnp.int32(2)), lax.axis_index("col"), lax.rem(row, jnp.int32(2))


def placed(kernel):
    def run(*refs):
        kernel(coordinates(), *refs)

    return run


def call(kernel, name, outs, inputs, flops=0, scratch=()):
    shapes = [(jax.ShapeDtypeStruct if name == "finish" else pltpu.VMEM)(shape, kind) for shape, kind in outs]
    weight = WEIGHTS.get(name, 1)
    moved = sum(x.size * x.dtype.itemsize for x in inputs) + sum(math.prod(s) * jnp.dtype(k).itemsize for s, k in outs)
    return pl.pallas_call(
        kernel,
        name=name,
        out_shape=shapes,
        in_specs=[SMEM if x.size == 4 else HBM if name == "orders" else VMEM for x in inputs],
        out_specs=[HBM if name == "finish" else VMEM] * len(shapes),
        scratch_shapes=list(scratch),
        cost_estimate=pl.CostEstimate(flops=int(flops * weight), bytes_accessed=int(moved * weight), transcendentals=0),
        compiler_params=pltpu.CompilerParams(vmem_limit_bytes=SOME_VMEM),
    )(*inputs)


def body(vectors_in, poles_one, roots_one, order_one, deflate_one, poles_two, roots_two, order_two, deflate_two):
    row_total = lax.axis_size("row")
    assert lax.axis_size("col") == 4
    row_place = lax.axis_index("row")
    col_place = lax.axis_index("col")
    local_rows, share = vectors_in.shape
    leaf = 4 * share
    width_one = 2 * leaf
    width_two = 4 * leaf
    columns = width_two // 4
    per_leaf = row_total // 4
    assert per_leaf % 2 == 0
    leaf_number = row_place // per_leaf
    pair = leaf_number // 2
    side = leaf_number % 2
    place = jnp.stack([pair, side, col_place, row_place % 2]).astype(jnp.int32)
    roots_two, order_two, poles_two, deflate_two = (
        a.reshape(1, width_two) for a in (roots_two, order_two, poles_two, deflate_two)
    )

    def along_col(x, moves):
        return lax.ppermute(x, "col", moves)

    rows = jnp.concatenate([vectors_in[0:1], vectors_in[local_rows - 1 :]], axis=0)
    rows = jnp.concatenate([rows] + [along_col(rows, [(i, i ^ k) for i in range(4)]) for k in (1, 2, 3)], axis=1)
    far = along_col(vectors_in, [(0, 2), (1, 3), (2, 0), (3, 1)])
    near = along_col(vectors_in, [(0, 1), (1, 0), (2, 3), (3, 2)])

    first_row, last_row = rows[0:1], rows[1:2]
    start = 2 * pair * per_leaf
    edges = jnp.concatenate(
        [
            jnp.where(row_place == start + per_leaf - 1, last_row, 0.0),
            jnp.where(row_place == start + per_leaf, first_row, 0.0),
            jnp.where(row_place == 2 * per_leaf - 1, last_row, jnp.where(row_place == 2 * per_leaf, first_row, 0.0)),
            jnp.zeros((5, leaf), F32),
        ],
        axis=0,
    )
    step = 1
    while step < 2 * per_leaf:
        edges = edges + lax.ppermute(edges, "row", [(i, i ^ step) for i in range(row_total)])
        step *= 2

    blocks = width_one // LANES
    raw = [poles_one, roots_one, order_one, deflate_one, poles_two, roots_two, order_two, deflate_two]
    raw = [pltpu.with_memory_space_constraint(x, pltpu.HBM) for x in raw]
    one_cols, two_cols, roots_one, flags_one, roots_two, flags_two = call(
        perm_kernel, "orders",
        [((LANES, 2 * blocks), F32)] * 2
        + [((1, width_one), F32), ((1, width_one), jnp.int32), ((1, columns), F32), ((1, columns), jnp.int32)],
        [place, *raw],
        scratch=[pltpu.VMEM(x.shape, x.dtype) for x in raw] + [pltpu.SemaphoreType.DMA((len(raw),))],
    )
    (sums,) = call(
        placed(norm_one_kernel), "norm_one", [((2, width_one), F32)],
        [edges, one_cols, roots_one], flops=10 * leaf * width_one,
        scratch=[pltpu.VMEM((2 * share // LANES, LANES, 8), F32)],
    )
    sums_there = lax.ppermute(sums, "row", [(i, i ^ 1) for i in range(row_total)])
    one_high, one_low = call(
        table_one_kernel, "table_one", [((leaf // 2, width_one), BF16)] * 2,
        [one_cols, roots_one], flops=10 * leaf * width_one,
    )
    (table_two,) = call(
        placed(table_two_kernel), "table_two", [((width_one, columns), F32)],
        [two_cols, roots_two], flops=10 * width_one * columns,
    )
    (weights,) = call(
        placed(weight_kernel), "weights", [((LANES, 2 * blocks + leaf // 2 // LANES), F32)],
        [sums, sums_there, edges, flags_one, one_cols, two_cols],
    )
    b_high, b_low, squares = call(
        scale_kernel, "scale", [((width_one, columns), BF16)] * 2 + [((1, columns), F32)],
        [weights, table_two], flops=10 * width_one * columns,
    )
    half_row = row_total // 2
    squares_far = lax.ppermute(squares, "row", [(i, (i + half_row) % row_total) for i in range(row_total)])
    own_mids, other_mids = [], []
    for part in range(2):
        pieces = PIECES[part]
        own = call(
            functools.partial(mid_kernel, part), "mid", [((share // pieces, columns), F32)] * pieces,
            [weights, one_high, one_low, b_high, b_low], flops=6 * share * width_one * columns,
        )
        own_mids.append(own)
        if part == 0:
            b_high, near, far = lax.optimization_barrier((b_high, near, far))
            last_end = along_col(far, [(1, 0), (2, 3)])
            last_middle = along_col(vectors_in, [(1, 2), (2, 1)])
        other_mids.append([lax.ppermute(x, "row", [(i, i ^ 1) for i in range(row_total)]) for x in own])
    (total,) = call(
        placed(apply_kernel), "apply", [((local_rows, columns), F32)],
        [*own_mids[0], *other_mids[0], vectors_in, far], flops=6 * local_rows * 2 * share * columns,
    )
    token, last_end, last_middle, total = lax.optimization_barrier((squares[:, :LANES], last_end, last_middle, total))
    token = lax.ppermute(token, "row", [(i, i ^ 1) for i in range(row_total)])
    total, token = lax.optimization_barrier((total, token))
    (merged,) = call(
        placed(finish_kernel), "finish", [((local_rows, columns), F32)],
        [near, last_end, last_middle, total, squares, squares_far, flags_two, *own_mids[1], *other_mids[1]],
        flops=6 * local_rows * 2 * share * columns,
        scratch=[pltpu.VMEM((local_rows, columns), F32), pltpu.SemaphoreType.DMA((4,))],
    )
    return merged


def solution(mesh):
    placed = (P("row", "col"), P(), P(), P(), P(), P(), P(), P(), P())
    return jax.shard_map(body, mesh=mesh, in_specs=placed, out_specs=P("row", "col"), check_vma=False)
```

```python
import functools
import math

import jax
import jax.numpy as jnp
from jax import lax
from jax.experimental import pallas as pl
from jax.experimental.pallas import tpu as pltpu
from jax.sharding import PartitionSpec as P

F32 = jnp.float32
BF16 = jnp.bfloat16
LANES = 128
SOME_VMEM = 14 * 1024 * 1024
ROWS, WIDTH = 32, 512
PIECES = (1, 2)
WEIGHTS = {"orders": 100, "table_one": 100, "table_two": 100, "norm_one": 100, "apply": 0.001, "mid_late": 6, "finish": 0.001}


def split(x):
    high = x.astype(BF16)
    return high, (x - high.astype(F32)).astype(BF16)


def dot3(a_high, a_low, b_high, b_low):
    dot = functools.partial(jnp.dot, preferred_element_type=F32)
    return dot(a_high, b_high) + dot(a_low, b_high) + dot(a_high, b_low)


def as_columns(row):
    count = row.shape[1] // LANES
    stacked = jnp.concatenate([row[:, LANES * b : LANES * (b + 1)] for b in range(count)], axis=0)
    return stacked.T


def permuted(order, low_bits, wanted, values):
    at_high = order >> 7 == wanted
    at_low = ((order & 127) == low_bits).astype(BF16)
    rows = jnp.concatenate([jnp.where(at_high, v, 0.0).astype(BF16) for v in values], axis=0)
    out = lax.dot_general(rows, at_low, (((1,), (1,)), ((), ())), preferred_element_type=F32)
    count = wanted.shape[0]
    return [out[count * i : count * (i + 1)] for i in range(len(values))]


def place_tables(order, poles, flags, wanted):
    span = order.shape[1]
    low_bits = lax.broadcasted_iota(jnp.int32, (LANES, span), 0)
    index = lax.broadcasted_iota(jnp.int32, (1, span), 1)
    first = poles.astype(BF16).astype(F32)
    second = (poles - first).astype(BF16).astype(F32)
    third = poles - first - second
    values = [first, second, third, (index >> 6).astype(F32), (index & 63).astype(F32), flags.astype(F32)]
    one, two, three, upper, lower, flag = permuted(order, low_bits, wanted, values)
    gone = flag > 0.5
    pole = jnp.where(gone, jnp.inf, one + two + three)
    target = jnp.where(gone, upper * 64.0 + lower, -1.0)
    return pole, target


def perm_kernel(place, *refs):
    given, outs, (held, arrived) = refs[:8], refs[8:14], (refs[14:22], refs[22])
    one_out, two_out, roots_one_out, flags_one_out, roots_two_out, flags_two_out = outs
    copies = [pltpu.make_async_copy(x, y, arrived.at[i]) for i, (x, y) in enumerate(zip(given, held))]
    for copy in copies:
        copy.start()
    for copy in copies:
        copy.wait()
    poles_one, roots_one, order_one, flags_one, poles_two, roots_two, order_two, flags_two = held
    pair, side, piece, core = place[0], place[1], place[2], place[3]
    blocks = order_one.shape[1] // LANES
    spot = lax.broadcasted_iota(jnp.int32, (blocks, 1), 0)
    half = blocks // 2
    per = half // 4
    late = spot - half // 2
    wanted_one = jnp.where(late < 0, side, 1 - side) * half
    wanted_one += (((spot % (half // 2)) // per) ^ piece ^ (2 * core)) * per + spot % per
    wanted_one = jnp.where(spot < half, wanted_one, -1)
    at = pl.ds(pair, 1)
    flags = flags_one[at, :]
    flags_one_out[...] = flags
    roots_one_out[...] = jnp.where(flags > 0, -jnp.inf, roots_one[at, :])
    pole, target = place_tables(order_one[at, :], poles_one[at, :], flags, wanted_one)
    one_out[...] = jnp.concatenate([pole, target], axis=0).T
    columns = roots_two_out.shape[1]
    lanes = pl.ds(pl.multiple_of(piece * columns, LANES), columns)
    flags = flags_two[:, lanes]
    flags_two_out[...] = flags
    roots_two_out[...] = jnp.where(flags > 0, -jnp.inf, roots_two[:, lanes])
    pole, target = place_tables(order_two[...], poles_two[...], flags_two[...], spot + pair * blocks)
    two_out[...] = jnp.concatenate([pole, target], axis=0).T


def inverse_gap(pole, target, roots, index):
    gap = pltpu.reciprocal(pole - roots, approx=True)
    return jnp.where(target == index, 1.0, gap)


def over_tiles(height, width, tile):
    for first in range(0, width, WIDTH):
        lanes = slice(first, first + WIDTH)
        for b in range(height // LANES):

            def step(i, _, b=b, lanes=lanes):
                near = pl.multiple_of(i * ROWS, ROWS)
                tile(b, pl.ds(near, ROWS), pl.ds(pl.multiple_of(b * LANES + near, ROWS), ROWS), lanes)
                return 0

            lax.fori_loop(0, LANES // ROWS, step, 0, unroll=LANES // ROWS)


def table_one_kernel(cols_ref, roots_ref, high_ref, low_ref):
    roots = roots_ref[...]
    index = lax.broadcasted_iota(jnp.int32, roots.shape, 1).astype(F32)
    blocks = cols_ref.shape[1] // 2

    def tile(b, near, rows, lanes):
        pole, target = cols_ref[near, b : b + 1], cols_ref[near, blocks + b : blocks + b + 1]
        high_ref[rows, lanes], low_ref[rows, lanes] = split(inverse_gap(pole, target, roots[:, lanes], index[:, lanes]))

    over_tiles(*high_ref.shape, tile)


def table_two_kernel(place, cols_ref, roots_ref, out_ref):
    roots = roots_ref[...]
    index = (lax.broadcasted_iota(jnp.int32, roots.shape, 1) + place[2] * out_ref.shape[1]).astype(F32)
    blocks = cols_ref.shape[1] // 2

    def tile(b, near, rows, lanes):
        pole, target = cols_ref[near, b : b + 1], cols_ref[near, blocks + b : blocks + b + 1]
        out_ref[rows, lanes] = inverse_gap(pole, target, roots[:, lanes], index[:, lanes])

    over_tiles(*out_ref.shape, tile)


def add_rows(total, x):
    for i in range(0, x.shape[0], 8):
        total = total + x[i : i + 8]
    return total


def norm_one_kernel(place, edge_ref, cols_ref, roots_ref, out_ref, edge_cols):
    pair, side, core = place[0], place[1], place[3]
    roots = roots_ref[...]
    width = roots.shape[1]
    index = lax.broadcasted_iota(jnp.int32, roots.shape, 1).astype(F32)
    blocks = cols_ref.shape[1] // 2
    share = edge_ref.shape[1] // 2
    edges = edge_ref[:, pl.ds(pl.multiple_of(core * share, LANES), share)]
    own = jnp.where(side == 0, edges[0:1], edges[1:2])
    other = jnp.where(side == 0, edges[1:2], edges[0:1])
    own_edge = jnp.where(side == 1 - pair, edges[2:3], 0.0)
    other_edge = jnp.where(side == 1 - pair, 0.0, edges[2:3])
    pad = jnp.zeros((4, share), F32)
    rows_all = jnp.concatenate([own, other, own_edge, other_edge, pad], axis=0)
    for b in range(share // LANES):
        edge_cols[b] = rows_all[:, LANES * b : LANES * (b + 1)].T
    for first in range(0, width, WIDTH):
        lanes = slice(first, first + WIDTH)
        carry = (jnp.zeros((8, WIDTH), F32), jnp.zeros((8, WIDTH), F32))
        for part in range(2):
            for b in range(share // LANES):
                block = part * (share // LANES) + b

                def step(i, carry, part=part, b=b, block=block, lanes=lanes):
                    rows = pl.ds(pl.multiple_of(i * ROWS, ROWS), ROWS)
                    target = cols_ref[rows, blocks + block : blocks + block + 1]
                    gap = pltpu.reciprocal(cols_ref[rows, block : block + 1] - roots[:, lanes], approx=True)
                    z = edge_cols[b, rows, part : part + 1]
                    edge = edge_cols[b, rows, 2 + part : 3 + part]
                    scaled = z * gap
                    weighed = edge * jnp.where(target == index[:, lanes], 1.0, scaled)
                    return add_rows(carry[0], scaled * scaled), add_rows(carry[1], weighed)

                carry = lax.fori_loop(0, LANES // ROWS, step, carry, unroll=LANES // ROWS)
        out_ref[0:1, lanes] = jnp.sum(carry[0], axis=0, keepdims=True)
        out_ref[1:2, lanes] = jnp.sum(carry[1], axis=0, keepdims=True)


def weight_kernel(place, here, there, edge_ref, flags_ref, one_cols, two_cols, out_ref):
    squares = here[0:1, :] + there[0:1, :]
    edge = here[1:2, :] + there[1:2, :]
    gone = flags_ref[...] > 0
    scale = as_columns(jnp.where(gone, 1.0, lax.rsqrt(squares + 1e-06)))
    blocks = two_cols.shape[1] // 2
    z_two = as_columns(edge) * scale
    row_gone = two_cols[:, blocks:] >= 0.0
    out_ref[:, 0:blocks] = scale * jnp.where(row_gone, 1.0, z_two)
    out_ref[:, blocks : 2 * blocks] = jnp.where(row_gone, 0.0, z_two)
    share = edge_ref.shape[1] // 2
    edges = edge_ref[:, pl.ds(pl.multiple_of(place[3] * share, LANES), share)]
    z_one = as_columns(jnp.where(place[1] == 0, edges[0:1], edges[1:2]))
    count = z_one.shape[1]
    row_gone = one_cols[:, blocks : blocks + count] >= 0.0
    out_ref[:, 2 * blocks : 2 * blocks + count] = jnp.where(row_gone, 1.0, z_one)


def scale_kernel(weights, two_ref, b_high, b_low, squares_ref):
    depth, columns = b_high.shape
    blocks = depth // LANES
    for first in range(0, columns, WIDTH):
        lanes = slice(first, first + WIDTH)
        squares = jnp.zeros((8, WIDTH), F32)
        for b in range(blocks):

            def step(i, squares, b=b, lanes=lanes):
                rows = pl.ds(pl.multiple_of(i * ROWS, ROWS), ROWS)
                to = pl.ds(pl.multiple_of(b * LANES + i * ROWS, ROWS), ROWS)
                table = two_ref[to, lanes]
                b_high[to, lanes], b_low[to, lanes] = split(table * weights[rows, b : b + 1])
                scaled = table * weights[rows, blocks + b : blocks + b + 1]
                return add_rows(squares, scaled * scaled)

            squares = lax.fori_loop(0, LANES // ROWS, step, squares, unroll=LANES // ROWS)
        squares_ref[:, lanes] = jnp.sum(squares, axis=0, keepdims=True)


def mid_kernel(part, weights, high_ref, low_ref, b_high, b_low, *outs):
    piece, columns = outs[0].shape
    height = piece * len(outs)
    blocks = b_high.shape[0] // LANES
    rows = slice(height * part, height * (part + 1))
    for first in range(0, columns, WIDTH):
        lanes = slice(first, first + WIDTH)
        mid = dot3(high_ref[rows, :], low_ref[rows, :], b_high[:, lanes], b_low[:, lanes])
        for i, out_ref in enumerate(outs):
            for begin in range(0, piece, LANES):
                count = min(LANES, piece)
                b, inner = divmod(piece * i + begin, LANES)
                at = 2 * blocks + part * (height // LANES) + b
                scale = weights[inner : inner + count, at : at + 1]
                out_ref[begin : begin + count, lanes] = mid[piece * i + begin : piece * i + begin + count] * scale


def apply_kernel(place, own_mid, other_mid, mine, far, out_ref):
    first = place[3] == 0
    own = split(jnp.where(first, mine[...], far[...]))
    other = split(jnp.where(first, far[...], mine[...]))
    for at in range(0, out_ref.shape[1], WIDTH):
        lanes = slice(at, at + WIDTH)
        out_ref[:, lanes] = dot3(*own, *split(own_mid[:, lanes])) + dot3(*other, *split(other_mid[:, lanes]))


def finish_kernel(place, near_ref, last_end, last_middle, total_ref, squares, squares_far, flags_ref, *refs):
    count = len(refs) // 2 - 1
    own_late, other_late, (out_ref, done, left) = refs[:count], refs[count : 2 * count], refs[2 * count :]
    scale = jnp.where(flags_ref[...] > 0, 1.0, lax.rsqrt(squares[...] + squares_far[...] + 1e-06))
    first = place[3] == 0
    near, last = near_ref[...], last_end[...] + last_middle[...]
    own, other = jnp.where(first, near, last), jnp.where(first, last, near)
    own_mid = split(jnp.concatenate([x[...] for x in own_late], axis=0))
    other_mid = split(jnp.concatenate([x[...] for x in other_late], axis=0))
    copies = []
    height = out_ref.shape[0] // left.shape[0]
    for i in range(left.shape[0]):
        rows = slice(height * i, height * (i + 1))
        term = dot3(*split(own[rows]), *own_mid) + dot3(*split(other[rows]), *other_mid)
        done[rows, :] = (total_ref[rows, :] + term) * scale
        copies.append(pltpu.make_async_copy(done.at[rows, :], out_ref.at[rows, :], left.at[i]))
        copies[-1].start()
    for copy in copies:
        copy.wait()


SMEM = pl.BlockSpec(memory_space=pltpu.SMEM)
VMEM = pl.BlockSpec(memory_space=pltpu.VMEM)
HBM = pl.BlockSpec(memory_space=pltpu.HBM)


def coordinates():
    per_leaf = lax.axis_size("row") // 4
    row = lax.axis_index("row")
    leaf = lax.div(row, jnp.int32(per_leaf))
    return lax.div(leaf, jnp.int32(2)), lax.rem(leaf, jnp.int32(2)), lax.axis_index("col"), lax.rem(row, jnp.int32(2))


def placed(kernel):
    def run(*refs):
        kernel(coordinates(), *refs)

    return run


def call(kernel, name, outs, inputs, flops=0, scratch=()):
    shapes = [(jax.ShapeDtypeStruct if name == "finish" else pltpu.VMEM)(shape, kind) for shape, kind in outs]
    weight = WEIGHTS.get(name, 1)
    moved = sum(x.size * x.dtype.itemsize for x in inputs) + sum(math.prod(s) * jnp.dtype(k).itemsize for s, k in outs)
    return pl.pallas_call(
        kernel,
        name=name,
        out_shape=shapes,
        in_specs=[SMEM if x.size == 4 else HBM if name == "orders" else VMEM for x in inputs],
        out_specs=[HBM if name == "finish" else VMEM] * len(shapes),
        scratch_shapes=list(scratch),
        cost_estimate=pl.CostEstimate(flops=int(flops * weight), bytes_accessed=int(moved * weight), transcendentals=0),
        compiler_params=pltpu.CompilerParams(vmem_limit_bytes=SOME_VMEM),
    )(*inputs)


def body(vectors_in, poles_one, roots_one, order_one, deflate_one, poles_two, roots_two, order_two, deflate_two):
    row_total = lax.axis_size("row")
    assert lax.axis_size("col") == 4
    row_place = lax.axis_index("row")
    col_place = lax.axis_index("col")
    local_rows, share = vectors_in.shape
    leaf = 4 * share
    width_one = 2 * leaf
    width_two = 4 * leaf
    columns = width_two // 4
    per_leaf = row_total // 4
    assert per_leaf % 2 == 0
    leaf_number = row_place // per_leaf
    pair = leaf_number // 2
    side = leaf_number % 2
    place = jnp.stack([pair, side, col_place, row_place % 2]).astype(jnp.int32)
    roots_two, order_two, poles_two, deflate_two = (
        a.reshape(1, width_two) for a in (roots_two, order_two, poles_two, deflate_two)
    )

    def along_col(x, moves):
        return lax.ppermute(x, "col", moves)

    rows = jnp.concatenate([vectors_in[0:1], vectors_in[local_rows - 1 :]], axis=0)
    rows = jnp.concatenate([rows] + [along_col(rows, [(i, i ^ k) for i in range(4)]) for k in (1, 2, 3)], axis=1)
    far = along_col(vectors_in, [(0, 2), (1, 3), (2, 0), (3, 1)])
    near = along_col(vectors_in, [(0, 1), (1, 0), (2, 3), (3, 2)])

    first_row, last_row = rows[0:1], rows[1:2]
    start = 2 * pair * per_leaf
    edges = jnp.concatenate(
        [
            jnp.where(row_place == start + per_leaf - 1, last_row, 0.0),
            jnp.where(row_place == start + per_leaf, first_row, 0.0),
            jnp.where(row_place == 2 * per_leaf - 1, last_row, jnp.where(row_place == 2 * per_leaf, first_row, 0.0)),
            jnp.zeros((5, leaf), F32),
        ],
        axis=0,
    )
    step = 1
    while step < 2 * per_leaf:
        edges = edges + lax.ppermute(edges, "row", [(i, i ^ step) for i in range(row_total)])
        step *= 2

    blocks = width_one // LANES
    raw = [poles_one, roots_one, order_one, deflate_one, poles_two, roots_two, order_two, deflate_two]
    raw = [pltpu.with_memory_space_constraint(x, pltpu.HBM) for x in raw]
    one_cols, two_cols, roots_one, flags_one, roots_two, flags_two = call(
        perm_kernel, "orders",
        [((LANES, 2 * blocks), F32)] * 2
        + [((1, width_one), F32), ((1, width_one), jnp.int32), ((1, columns), F32), ((1, columns), jnp.int32)],
        [place, *raw],
        scratch=[pltpu.VMEM(x.shape, x.dtype) for x in raw] + [pltpu.SemaphoreType.DMA((len(raw),))],
    )
    (sums,) = call(
        placed(norm_one_kernel), "norm_one", [((2, width_one), F32)],
        [edges, one_cols, roots_one], flops=10 * leaf * width_one,
        scratch=[pltpu.VMEM((2 * share // LANES, LANES, 8), F32)],
    )
    sums_there = lax.ppermute(sums, "row", [(i, i ^ 1) for i in range(row_total)])
    one_high, one_low = call(
        table_one_kernel, "table_one", [((leaf // 2, width_one), BF16)] * 2,
        [one_cols, roots_one], flops=10 * leaf * width_one,
    )
    (table_two,) = call(
        placed(table_two_kernel), "table_two", [((width_one, columns), F32)],
        [two_cols, roots_two], flops=10 * width_one * columns,
    )
    (weights,) = call(
        placed(weight_kernel), "weights", [((LANES, 2 * blocks + leaf // 2 // LANES), F32)],
        [sums, sums_there, edges, flags_one, one_cols, two_cols],
    )
    b_high, b_low, squares = call(
        scale_kernel, "scale", [((width_one, columns), BF16)] * 2 + [((1, columns), F32)],
        [weights, table_two], flops=10 * width_one * columns,
    )
    half_row = row_total // 2
    squares_far = lax.ppermute(squares, "row", [(i, (i + half_row) % row_total) for i in range(row_total)])
    own_mids, other_mids = [], []
    for part in range(2):
        pieces = PIECES[part]
        own = call(
            functools.partial(mid_kernel, part), ("mid", "mid_late")[part], [((share // pieces, columns), F32)] * pieces,
            [weights, one_high, one_low, b_high, b_low], flops=6 * share * width_one * columns,
        )
        own_mids.append(own)
        if part == 0:
            b_high, near, far = lax.optimization_barrier((b_high, near, far))
            last_end = along_col(far, [(1, 0), (2, 3)])
            last_middle = along_col(vectors_in, [(1, 2), (2, 1)])
        other_mids.append([lax.ppermute(x, "row", [(i, i ^ 1) for i in range(row_total)]) for x in own])
    (total,) = call(
        placed(apply_kernel), "apply", [((local_rows, columns), F32)],
        [*own_mids[0], *other_mids[0], vectors_in, far], flops=6 * local_rows * 2 * share * columns,
    )
    token, last_end, last_middle, total = lax.optimization_barrier((squares[:, :LANES], last_end, last_middle, total))
    token = lax.ppermute(token, "row", [(i, i ^ 1) for i in range(row_total)])
    total, token = lax.optimization_barrier((total, token))
    (merged,) = call(
        placed(finish_kernel), "finish", [((local_rows, columns), F32)],
        [near, last_end, last_middle, total, squares, squares_far, flags_two, *own_mids[1], *other_mids[1]],
        flops=6 * local_rows * 2 * share * columns,
        scratch=[pltpu.VMEM((local_rows, columns), F32), pltpu.SemaphoreType.DMA((4,))],
    )
    return merged


def solution(mesh):
    placed = (P("row", "col"), P(), P(), P(), P(), P(), P(), P(), P())
    return jax.shard_map(body, mesh=mesh, in_specs=placed, out_specs=P("row", "col"), check_vma=False)
```
